256 devices in a mesh: ctx: 64 (over x, z, core), head: 4 (over y).
Axes of the slice: x: 4, y: 4, z: 8, core: 2. Of those that a mesh axis runs over, the one named last changes fastest.
Arguments:
- queries: bfloat16 [32768, 2048], P(('ctx', 'head')), may hold values from -32 to 32
- key_states: bfloat16 [32768, 512], P(('ctx', 'head')), may hold values from -12 to 12
- value_states: bfloat16 [32768, 512], P(('ctx', 'head')), may hold values from -6 to 6
- out_grad: bfloat16 [32768, 2048], P(('ctx', 'head')), may hold values from -6 to 6
- lengths: int32 [21], replicated, may hold values from 1 to 3072, 32768 in all
Outputs:
- attended: bfloat16 [32768, 2048], P(('ctx', 'head'))
- query_grad: bfloat16 [32768, 2048], P(('ctx', 'head'))
- key_grad: bfloat16 [32768, 512], P(('ctx', 'head'))
- value_grad: bfloat16 [32768, 512], P(('ctx', 'head'))
The draws below stay inside these ranges and needn't reach their ends.
Inputs may be any that keep to these rules, and one draw needn't show every extreme that they name: lengths of the 21 documents packed in order; they sum to 32768 and the longest has exactly 3072 tokens.
All inputs are finite; a program needn't handle non-finite values.
Results may differ from the reference program's by a relative error of at most 0.039.
Values may be sent and summed in bfloat16 or wider, within the bound.
A program may use at most 128 MiB of HBM per device.

```python
import math
import jax
import jax.numpy as jnp
import numpy as np
from jax import lax

HD = 128
HEADS = 16
KV_HEADS = 4
TOK_DEV = 512
SPAN = 6
DOC_MOST = 3072
TOKENS = 32768
NDOCS = 21


def shared_pair(key, strength):
    positions = jnp.arange(TOKENS, dtype=jnp.int32)
    key_base = jax.random.truncated_normal(jax.random.fold_in(key, 11), -4.0, 4.0, (TOKENS, KV_HEADS * HD), jnp.float32)
    query_base = jax.random.truncated_normal(jax.random.fold_in(key, 12), -4.0, 4.0, (TOKENS, HEADS * HD), jnp.float32)
    chosen = positions % 97 == 5
    before = positions % 97 == 4
    near_copy = jnp.roll(key_base, -1, axis=0) * 0.99
    key_drawn = jnp.where(before[:, None], near_copy, key_base)
    marked = (chosen | before)[:, None]
    key_mixed = jnp.where(marked, key_drawn, key_drawn)
    levels = strength * (1.0 + 0.5 * (positions // 97 % 4).astype(jnp.float32))
    aligned = jnp.repeat(key_drawn.reshape(TOKENS, KV_HEADS, 1, HD), HEADS // KV_HEADS, axis=2).reshape(TOKENS, HEADS * HD)
    aligned = aligned * levels[:, None]
    query_mixed = jnp.where(chosen[:, None] & (strength > 0.0), aligned, query_base)
    return (query_mixed, key_mixed)


def draw_queries(key, part):
    drawn_pair = shared_pair(key, 0.0)
    return drawn_pair[0].astype(jnp.bfloat16)


def draw_key_states(key, part):
    drawn_pair = shared_pair(key, 0.0)
    return drawn_pair[1].astype(jnp.bfloat16)


def shard_levels(own_key, shape, pieces, smallest, top_value):
    level = 1.0
    for position, blocks in pieces:
        draws = jax.random.uniform(jax.random.fold_in(jax.random.fold_in(own_key, 6), position), (blocks,), jnp.float32, smallest / len(pieces), top_value / len(pieces))
        level = level * jnp.repeat(jnp.exp(draws), shape[position] // blocks).reshape((-1,) + (1,) * (len(shape) - 1 - position))
    return level


def profile(count, total, limit, skew):
    portions = [(1 << 20) // math.isqrt(standing ** skew) + 1 for standing in range(2, count + 1)]
    rest, counts = total - limit - (count - 1), [1] * (count - 1)
    while rest > 0:
        movable = [i for i in range(count - 1) if counts[i] < limit]
        whole, budget = sum([portions[i] for i in movable]), rest
        for i in movable:
            addition = min(limit - counts[i], max(1, budget * portions[i] // whole), rest)
            counts[i] = counts[i] + addition
            rest = rest - addition
    return np.array([limit] + counts)


def uneven(key, amount, total, reach, lean):
    if amount == 2:
        one = jax.random.randint(key, (), max(1, total - reach), min(reach, total - 1) + 1)
        return jnp.stack([one, total - one])
    tallies = jnp.asarray(profile(amount, total, reach, lean), jnp.int32)
    pairs = (amount - 1) // 2
    giver, taker = tallies[1:1 + 2 * pairs:2], tallies[2:2 + 2 * pairs:2]
    margin = jnp.minimum(giver - 1, reach - taker)
    shifted = jax.random.randint(jax.random.fold_in(key, 1), (pairs,), 0, 1 << 20) % (margin + 1)
    tallies = tallies.at[1:1 + 2 * pairs:2].set(giver - shifted).at[2:2 + 2 * pairs:2].set(taker + shifted)
    return tallies[jax.random.permutation(jax.random.fold_in(key, 2), amount)]


def centred(key, extent, deviation, limit, shards=(), kind=jnp.bfloat16):
    array = deviation * jax.random.normal(key, extent, jnp.float32)
    if shards:
        array = array * shard_levels(key, extent, shards, -0.22, 0.18)
    return jnp.clip(array, -limit, limit).astype(kind)


def setup_inputs(seed: int = 0) -> dict:
    arg_keys = jax.random.split(jax.random.key(seed), 6)
    queries = draw_queries(jax.random.fold_in(arg_keys[5], 71), 0)
    key_states = draw_key_states(jax.random.fold_in(arg_keys[5], 71), 0)
    value_states = centred(arg_keys[2], (TOKENS, KV_HEADS * HD), 1.0, 6.0, ((0, 256),))
    out_grad = centred(arg_keys[3], (TOKENS, HEADS * HD), 1.0, 6.0, ((0, 256),))
    lengths = uneven(arg_keys[4], NDOCS, TOKENS, DOC_MOST, 2).astype(jnp.int32)
    return dict(queries=queries, key_states=key_states, value_states=value_states, out_grad=out_grad, lengths=lengths)


def doc_of(lengths, positions):
    doc_ends = jnp.cumsum(lengths)
    return jnp.sum((positions[:, None] >= doc_ends[None, :]).astype(jnp.int32), axis=1)


def block_terms(block_index, queries, key_pad, value_pad, lengths):
    group_size = HEADS // KV_HEADS
    window = (SPAN + 1) * TOK_DEV
    row_start = (block_index * TOK_DEV).astype(jnp.int32)
    q_block = lax.dynamic_slice_in_dim(queries, row_start, TOK_DEV, 0).reshape(TOK_DEV, KV_HEADS, group_size, HD)
    key_window = lax.dynamic_slice_in_dim(key_pad, row_start, window, 0).reshape(window, KV_HEADS, HD)
    value_window = lax.dynamic_slice_in_dim(value_pad, row_start, window, 0).reshape(window, KV_HEADS, HD)
    query_pos = row_start + jnp.arange(TOK_DEV, dtype=jnp.int32)
    key_pos = row_start - SPAN * TOK_DEV + jnp.arange(window, dtype=jnp.int32)
    allowed = (key_pos[None, :] >= 0) & (key_pos[None, :] <= query_pos[:, None])
    allowed = allowed & (doc_of(lengths, query_pos)[:, None] == doc_of(lengths, key_pos)[None, :])
    logits = (HD ** -0.5) * jnp.einsum("qkgd,wkd->kgqw", q_block.astype(jnp.float32), key_window.astype(jnp.float32))
    logits = jnp.where(allowed[None, None], logits, -1e30)
    running_max = jnp.max(logits, axis=-1, keepdims=True)
    log_total = running_max + jnp.log(jnp.sum(jnp.exp(logits - running_max), axis=-1, keepdims=True))
    weights = jnp.exp(logits - log_total)
    return q_block, key_window, value_window, weights, row_start


def reference(queries, key_states, value_states, out_grad, lengths):
    group_size = HEADS // KV_HEADS
    window = (SPAN + 1) * TOK_DEV
    pad_rows = SPAN * TOK_DEV
    score_scale = HD ** -0.5
    zero_rows = jnp.zeros((pad_rows, KV_HEADS * HD), key_states.dtype)
    key_pad = jnp.concatenate([zero_rows, key_states], axis=0)
    value_pad = jnp.concatenate([zero_rows, value_states], axis=0)
    block_ids = jnp.arange(TOKENS // TOK_DEV, dtype=jnp.int32)

    def forward(block_index):
        q_block, key_window, value_window, weights, row_start = block_terms(block_index, queries, key_pad, value_pad, lengths)
        rounded = lax.optimization_barrier(weights.astype(jnp.bfloat16)).astype(jnp.float32)
        mixture = jnp.einsum("kgqw,wkd->qkgd", rounded, value_window.astype(jnp.float32))
        return mixture.astype(jnp.bfloat16).reshape(TOK_DEV, HEADS * HD)

    attended = lax.map(forward, block_ids).reshape(TOKENS, HEADS * HD)

    def backward(carried, block_index):
        dk_pad, dv_pad = carried
        q_block, key_window, value_window, weights, row_start = block_terms(block_index, queries, key_pad, value_pad, lengths)
        out_block = lax.dynamic_slice_in_dim(attended, row_start, TOK_DEV, 0).reshape(TOK_DEV, KV_HEADS, group_size, HD).astype(jnp.float32)
        grad_block = lax.dynamic_slice_in_dim(out_grad, row_start, TOK_DEV, 0).reshape(TOK_DEV, KV_HEADS, group_size, HD).astype(jnp.float32)
        rounded = lax.optimization_barrier(weights.astype(jnp.bfloat16)).astype(jnp.float32)
        delta_row = jnp.einsum("qkgd,qkgd->kgq", grad_block, out_block)
        dv_window = jnp.einsum("kgqw,qkgd->wkd", rounded, grad_block)
        prob_grad = jnp.einsum("qkgd,wkd->kgqw", grad_block, value_window.astype(jnp.float32))
        logit_grad = weights * (prob_grad - delta_row[..., None])
        logit_grad = lax.optimization_barrier(logit_grad.astype(jnp.bfloat16)).astype(jnp.float32)
        dq_block = score_scale * jnp.einsum("kgqw,wkd->qkgd", logit_grad, key_window.astype(jnp.float32))
        dk_window = score_scale * jnp.einsum("kgqw,qkgd->wkd", logit_grad, q_block.astype(jnp.float32))
        dk_old = lax.dynamic_slice_in_dim(dk_pad, row_start, window, 0)
        dv_old = lax.dynamic_slice_in_dim(dv_pad, row_start, window, 0)
        dk_pad = lax.dynamic_update_slice_in_dim(dk_pad, dk_old + dk_window.reshape(window, KV_HEADS * HD), row_start, 0)
        dv_pad = lax.dynamic_update_slice_in_dim(dv_pad, dv_old + dv_window.reshape(window, KV_HEADS * HD), row_start, 0)
        return (dk_pad, dv_pad), dq_block.astype(jnp.bfloat16).reshape(TOK_DEV, HEADS * HD)

    start_pads = (jnp.zeros((pad_rows + TOKENS, KV_HEADS * HD), jnp.float32), jnp.zeros((pad_rows + TOKENS, KV_HEADS * HD), jnp.float32))
    (dk_pad, dv_pad), dq_blocks = lax.scan(backward, start_pads, block_ids)
    query_grad = dq_blocks.reshape(TOKENS, HEADS * HD)
    key_grad = dk_pad[pad_rows:].astype(jnp.bfloat16)
    value_grad = dv_pad[pad_rows:].astype(jnp.bfloat16)
    return attended, query_grad, key_grad, value_grad
```

```python
import functools

import jax
import jax.numpy as jnp
import numpy as np
from jax import lax
from jax.experimental import pallas as pl
from jax.experimental.pallas import tpu as pltpu
from jax.sharding import PartitionSpec as P

HD = 128
SPAN = 6
TOK = 512
SLOT = 128
GROUP = 4
HOPS = 3
WINDOW = (SPAN + 1) * TOK
NDOCS = 21
TILE = 256
KEYS = 256
SCALE = HD ** (-0.5)
SCALE2 = float(HD ** (-0.5) * np.log2(np.e))
MESH = pl.DeviceIdType.MESH
BF16 = jnp.bfloat16
F32 = jnp.float32


def cols(index, width):
    return pl.ds(pl.multiple_of(index * width, width), width)


def places():
    me = lax.axis_index("ctx")
    y = lax.axis_index("head")
    count = lax.axis_size("ctx")
    core = lax.rem(me, 2)
    sibling = me + 1 - 2 * core
    after = lax.rem(me + 2, count)
    before = lax.rem(me + count - 2, count)
    return me, y, core, sibling, after, before


def greet(me, y, sibling, after, before):
    barrier = pltpu.get_barrier_semaphore()
    partners = [(me, lax.rem(y + r, 4)) for r in range(1, 4)]
    partners += [(sibling, y), (after, y), (before, y)]
    for partner in partners:
        pl.semaphore_signal(barrier, inc=1, device_id=partner, device_id_type=MESH)
    pl.semaphore_wait(barrier, len(partners))


def remote(src, dst, send, recv, device):
    return pltpu.make_async_remote_copy(
        src_ref=src, dst_ref=dst, send_sem=send, recv_sem=recv, device_id=device, device_id_type=MESH
    )


def gather_kernel(
    q_ref, k_ref, v_ref, g_ref, qh_ref, gh_ref, kv_ref,
    local_sem, kv_send, kv_recv, qg_send, qg_recv, ring_send, ring_recv, sib_send, sib_recv,
):
    me, y, core, sibling, after, before = places()
    own = 2 * HOPS + core
    local = [
        pltpu.make_async_copy(k_ref.at[:, cols(y, HD)], kv_ref.at[own, y, :, 0:HD], local_sem.at[0]),
        pltpu.make_async_copy(v_ref.at[:, cols(y, HD)], kv_ref.at[own, y, :, HD:2 * HD], local_sem.at[1]),
        pltpu.make_async_copy(q_ref.at[:, cols(y, GROUP * HD)], qh_ref.at[y], local_sem.at[2]),
        pltpu.make_async_copy(g_ref.at[:, cols(y, GROUP * HD)], gh_ref.at[y], local_sem.at[3]),
    ]
    for copy in local:
        copy.start()
    greet(me, y, sibling, after, before)

    kv_copies, qg_copies = {}, {}
    for r in range(1, 4):
        peer = lax.rem(y + r, 4)
        for part, ref in enumerate((k_ref, v_ref)):
            kv_copies[r, part] = remote(
                ref.at[:, cols(peer, HD)],
                kv_ref.at[own, y, :, part * HD:(part + 1) * HD],
                kv_send.at[r - 1, part], kv_recv.at[r - 1, part], (me, peer),
            )
            kv_copies[r, part].start()

    ring, sib = {}, {}

    def forward(distance, r):
        slot = lax.rem(y + 4 - r, 4)
        here = 2 * (HOPS - distance) + core
        if distance < HOPS:
            ring[distance, r] = remote(
                kv_ref.at[here, slot], kv_ref.at[here - 2, slot],
                ring_send.at[distance, r], ring_recv.at[distance, r], (after, y),
            )
            ring[distance, r].start()
        sib[distance, r] = remote(
            kv_ref.at[here, slot], kv_ref.at[here, slot],
            sib_send.at[distance, r], sib_recv.at[distance, r], (sibling, y),
        )
        sib[distance, r].start()

    local[0].wait()
    local[1].wait()
    forward(0, 0)
    for r in range(1, 4):
        peer = lax.rem(y + r, 4)
        for part, (ref, landing) in enumerate(((q_ref, qh_ref), (g_ref, gh_ref))):
            qg_copies[r, part] = remote(
                ref.at[:, cols(peer, GROUP * HD)], landing.at[y],
                qg_send.at[r - 1, part], qg_recv.at[r - 1, part], (me, peer),
            )
            qg_copies[r, part].start()
    for r in range(1, 4):
        kv_copies[r, 0].wait_recv()
        kv_copies[r, 1].wait_recv()
        forward(0, r)
    for distance in range(1, HOPS + 1):
        for r in range(4):
            ring[distance - 1, r].wait_recv()
            forward(distance, r)
    for copy in local[2:]:
        copy.wait()
    for copy in kv_copies.values():
        copy.wait_send()
    for copy in qg_copies.values():
        copy.wait()
    for copy in ring.values():
        copy.wait_send()
    for copy in sib.values():
        copy.wait()


def over(left, right, a, b):
    return lax.dot_general(left, right, (((a,), (b,)), ((), ())), preferred_element_type=F32)


def attention_kernel(len_ref, q_ref, g_ref, kv_ref, o_ref, dq_ref, dkv_ref, logits, weights, qs, gs, total):
    shard = lax.axis_index("ctx")
    base0 = lax.rem(shard, 2) * TOK
    first = shard * TOK - SPAN * TOK
    blocks = (SPAN * TOK + TILE) // KEYS
    width = GROUP * TILE
    slots = TILE // SLOT
    total[...] = jnp.zeros_like(total)
    for t in range(TOK // TILE):
        base = base0 + t * TILE
        for h in range(GROUP):
            for s in range(slots):
                row = h * TILE + s * SLOT
                qs[row:row + SLOT, :] = q_ref[t * slots + s, :, h * HD:(h + 1) * HD]
        local_pos = lax.broadcasted_iota(jnp.int32, (1, TILE), 1) + (SPAN * TOK + t * TILE)

        def later_start(d, carried):
            begin, start = carried
            at = begin - first
            return begin + len_ref[d], jnp.where(local_pos >= at, at, start)

        _, start = lax.fori_loop(
            0, NDOCS, later_start, (jnp.int32(0), jnp.zeros((1, TILE), jnp.int32) - first)
        )
        start = jnp.concatenate([start] * GROUP, axis=1)
        query_pos = jnp.concatenate([local_pos] * GROUP, axis=1)
        top = jnp.full((8, width), -1e30, F32)
        for b in range(blocks):
            rows = pl.ds(pl.multiple_of(base + b * KEYS, KEYS), KEYS)
            s = over(kv_ref[rows, 0:HD], qs[...], 1, 1)
            key_pos = lax.broadcasted_iota(jnp.int32, (KEYS, width), 0) + (t * TILE + b * KEYS)
            allowed = key_pos >= start
            if (b + 1) * KEYS > SPAN * TOK:
                allowed = allowed & (key_pos <= query_pos)
            s = jnp.where(allowed, s, -1e30)
            logits[b * KEYS:(b + 1) * KEYS, :] = s
            top = jnp.maximum(top, jnp.max(s.reshape(KEYS // 8, 8, width), axis=0))
        top = jnp.max(top, axis=0, keepdims=True) * SCALE2
        norm = jnp.zeros((8, width), F32)
        out = jnp.zeros((HD, width), F32)
        for b in range(blocks):
            rows = pl.ds(pl.multiple_of(base + b * KEYS, KEYS), KEYS)
            e = jnp.exp2(logits[b * KEYS:(b + 1) * KEYS, :] * SCALE2 - top)
            norm = norm + jnp.sum(e.reshape(KEYS // 8, 8, width), axis=0)
            e = e.astype(BF16)
            weights[b * KEYS:(b + 1) * KEYS, :] = e
            out = out + over(kv_ref[rows, HD:2 * HD], e, 0, 0)
        inverse = 1.0 / jnp.sum(norm, axis=0, keepdims=True)
        out = (out * inverse).astype(BF16)
        out_rows = out.T
        grads = []
        for h in range(GROUP):
            for s in range(slots):
                row = h * TILE + s * SLOT
                o_ref[t * slots + s, :, h * HD:(h + 1) * HD] = out_rows[row:row + SLOT, :]
                grads.append(g_ref[t * slots + s, :, h * HD:(h + 1) * HD].T)
        grad = (jnp.concatenate(grads, axis=1).astype(F32) * inverse).astype(BF16)
        delta = jnp.sum(grad.astype(F32) * out.astype(F32), axis=0, keepdims=True)
        gs[...] = grad.T
        dq = jnp.zeros((HD, width), F32)
        for b in range(blocks):
            rows = pl.ds(pl.multiple_of(base + b * KEYS, KEYS), KEYS)
            into = pl.ds(t * TILE + b * KEYS, KEYS)
            dp = over(kv_ref[rows, HD:2 * HD], gs[...], 1, 1)
            e = weights[b * KEYS:(b + 1) * KEYS, :]
            ds = (e.astype(F32) * (dp - delta)).astype(BF16)
            total[into, 0:HD] += over(ds, qs[...], 1, 0)
            total[into, HD:2 * HD] += over(e, gs[...], 1, 0)
            dq = dq + over(kv_ref[rows, 0:HD], ds, 0, 0)
        dq_rows = (dq * SCALE).astype(BF16).T
        for h in range(GROUP):
            for s in range(slots):
                row = h * TILE + s * SLOT
                dq_ref[t * slots + s, :, h * HD:(h + 1) * HD] = dq_rows[row:row + SLOT, :]
    dkv_ref[:, 0:HD] = (total[:, 0:HD] * SCALE).astype(BF16)
    dkv_ref[:, HD:2 * HD] = total[:, HD:2 * HD].astype(BF16)


def scatter_kernel(
    o_ref, dq_ref, dkv_ref, att_ref, dqo_ref, dk_ref, dv_ref,
    sib_buf, ring_out, ring_in, final,
    local_sem, od_send, od_recv, sib_send, sib_recv, ring_send, ring_recv, fin_send, fin_recv,
):
    me, y, core, sibling, after, before = places()
    local = [
        pltpu.make_async_copy(o_ref.at[y], att_ref.at[:, cols(y, GROUP * HD)], local_sem.at[0]),
        pltpu.make_async_copy(dq_ref.at[y], dqo_ref.at[:, cols(y, GROUP * HD)], local_sem.at[1]),
    ]
    for copy in local:
        copy.start()
    missing = HOPS * (1 - core)
    sib_buf[missing] = jnp.zeros_like(sib_buf[0])
    greet(me, y, sibling, after, before)

    sib = []
    for n in range(HOPS):
        for r in range(1, 5):
            slot = lax.rem(y + r, 4)
            sib.append(remote(
                dkv_ref.at[2 * n + 1, slot], sib_buf.at[HOPS - n - core, slot],
                sib_send.at[n, r - 1], sib_recv.at[n, r - 1], (sibling, y),
            ))
    for copy in sib:
        copy.start()
    od = []
    for r in range(1, 4):
        peer = lax.rem(y + r, 4)
        for part, (ref, landing) in enumerate(((o_ref, att_ref), (dq_ref, dqo_ref))):
            od.append(remote(
                ref.at[peer], landing.at[:, cols(y, GROUP * HD)],
                od_send.at[r - 1, part], od_recv.at[r - 1, part], (me, peer),
            ))
            od[-1].start()
    for copy in sib:
        copy.wait_recv()

    ring, fin = {}, []
    for distance in range(HOPS, -1, -1):
        for r in range(1, 5):
            slot = lax.rem(y + r, 4)
            value = dkv_ref[2 * (HOPS - distance), slot].astype(F32) + sib_buf[distance, slot].astype(F32)
            if distance < HOPS:
                ring[distance + 1, r].wait_recv()
                value = value + ring_in[distance, slot].astype(F32)
            value = value.astype(BF16)
            if distance > 0:
                ring_out[distance - 1, slot] = value
                ring[distance, r] = remote(
                    ring_out.at[distance - 1, slot], ring_in.at[distance - 1, slot],
                    ring_send.at[distance - 1, r - 1], ring_recv.at[distance - 1, r - 1], (before, y),
                )
                ring[distance, r].start()
            elif r < 4:
                final[slot] = value
                for part, landing in enumerate((dk_ref, dv_ref)):
                    fin.append(remote(
                        final.at[slot, :, part * HD:(part + 1) * HD], landing.at[:, cols(y, HD)],
                        fin_send.at[r - 1, part], fin_recv.at[r - 1, part], (me, slot),
                    ))
                    fin[-1].start()
            else:
                final[slot] = value
                for part, landing in enumerate((dk_ref, dv_ref)):
                    copy = pltpu.make_async_copy(
                        final.at[slot, :, part * HD:(part + 1) * HD], landing.at[:, cols(y, HD)],
                        local_sem.at[2 + part],
                    )
                    copy.start()
                    local.append(copy)
    for copy in local:
        copy.wait()
    for copy in sib:
        copy.wait_send()
    for copy in ring.values():
        copy.wait_send()
    for copy in od + fin:
        copy.wait()


def shards(queries, key_states, value_states, out_grad, lengths):
    hbm = pl.BlockSpec(memory_space=pl.ANY)
    vmem = pl.BlockSpec(memory_space=pltpu.VMEM)
    smem = pl.BlockSpec(memory_space=pltpu.SMEM)
    dma = pltpu.SemaphoreType.DMA
    by_head = jax.ShapeDtypeStruct((4, SLOT, GROUP * HD), BF16)
    q_head, g_head, kv = pl.pallas_call(
        gather_kernel,
        name="gather",
        out_shape=(by_head, by_head, jax.ShapeDtypeStruct((2 * HOPS + 2, 4, SLOT, 2 * HD), BF16)),
        in_specs=[hbm] * 4,
        out_specs=(hbm,) * 3,
        scratch_shapes=[
            dma((4,)), dma((3, 2)), dma((3, 2)), dma((3, 2)), dma((3, 2)),
            dma((HOPS, 4)), dma((HOPS, 4)), dma((HOPS + 1, 4)), dma((HOPS + 1, 4)),
        ],
        compiler_params=pltpu.CompilerParams(collective_id=0, has_side_effects=True),
    )(queries, key_states, value_states, out_grad)

    span = SPAN * TOK + TILE
    o, dq, dkv = pl.pallas_call(
        attention_kernel,
        name="attention",
        out_shape=(by_head, by_head, jax.ShapeDtypeStruct((WINDOW, 2 * HD), BF16)),
        in_specs=[smem] + [vmem] * 3,
        out_specs=(vmem,) * 3,
        scratch_shapes=[
            pltpu.VMEM((span, GROUP * TILE), F32),
            pltpu.VMEM((span, GROUP * TILE), BF16),
            pltpu.VMEM((GROUP * TILE, HD), BF16),
            pltpu.VMEM((GROUP * TILE, HD), BF16),
            pltpu.VMEM((WINDOW, 2 * HD), F32),
        ],
        compiler_params=pltpu.CompilerParams(vmem_limit_bytes=56 * 2**20),
    )(lengths, q_head, g_head, kv.reshape((2 * HOPS + 2) * TOK, 2 * HD))

    block = (4, SLOT, 2 * HD)
    return pl.pallas_call(
        scatter_kernel,
        name="scatter",
        out_shape=(
            jax.ShapeDtypeStruct((SLOT, 4 * GROUP * HD), BF16),
            jax.ShapeDtypeStruct((SLOT, 4 * GROUP * HD), BF16),
            jax.ShapeDtypeStruct((SLOT, 4 * HD), BF16),
            jax.ShapeDtypeStruct((SLOT, 4 * HD), BF16),
        ),
        in_specs=[hbm, hbm, vmem],
        out_specs=(hbm,) * 4,
        scratch_shapes=[
            pltpu.VMEM((HOPS + 1,) + block, BF16),
            pltpu.VMEM((HOPS,) + block, BF16),
            pltpu.VMEM((HOPS,) + block, BF16),
            pltpu.VMEM(block, BF16),
            dma((4,)), dma((3, 2)), dma((3, 2)), dma((HOPS, 4)), dma((HOPS, 4)),
            dma((HOPS, 4)), dma((HOPS, 4)), dma((3, 2)), dma((3, 2)),
        ],
        compiler_params=pltpu.CompilerParams(
            collective_id=1, has_side_effects=True, vmem_limit_bytes=32 * 2**20
        ),
    )(o, dq, dkv.reshape((SPAN + 1,) + block))


def solution(mesh):
    rows = P(("ctx", "head"), None)
    return jax.shard_map(
        shards, mesh=mesh, in_specs=(rows,) * 4 + (P(),), out_specs=(rows,) * 4, check_vma=False
    )
```

```python
import jax
import jax.numpy as jnp
import numpy as np
from jax import lax
from jax.experimental import pallas as pl
from jax.experimental.pallas import tpu as pltpu
from jax.sharding import PartitionSpec as P

HD = 128
SPAN = 6
TOK = 512
SLOT = 128
GROUP = 4
HOPS = 3
NDOCS = 21
TILE = 256
TILES = TOK // TILE
SUBS = 2 * (SPAN + 1)
WIDTH = GROUP * TILE
SCALE = HD ** (-0.5)
SCALE2 = float(HD ** (-0.5) * np.log2(np.e))
MESH = pl.DeviceIdType.MESH
BF16 = jnp.bfloat16
F32 = jnp.float32


def cols(index, width):
    return pl.ds(pl.multiple_of(index * width, width), width)


def over(left, right, a, b):
    return lax.dot_general(left, right, (((a,), (b,)), ((), ())), preferred_element_type=F32)


def remote(src, dst, send, recv, device):
    return pltpu.make_async_remote_copy(
        src_ref=src, dst_ref=dst, send_sem=send, recv_sem=recv, device_id=device, device_id_type=MESH
    )


def kernel(
    len_ref, q_ref, k_ref, v_ref, g_ref, att_ref, dqo_ref, dk_ref, dv_ref,
    kv, qh, gh, qs, gt, weights, logits, tops, sums, outs, dqs, gst, gs,
    o_buf, dq_buf, sib_out, sib_in, ring_out, ring_in, own_buf, final,
    local_sem, kv_send, kv_recv, qg_send, qg_recv, ring_send, ring_recv, sib_send, sib_recv,
    od_send, od_recv, back_sib_send, back_sib_recv, back_send, back_recv, fin_send, fin_recv,
):
    me = lax.axis_index("ctx")
    y = lax.axis_index("head")
    count = lax.axis_size("ctx")
    core = lax.rem(me, 2)
    sibling = (me + 1 - 2 * core, y)
    after = (lax.rem(me + 2, count), y)
    before = (lax.rem(me + count - 2, count), y)
    peers = [(me, lax.rem(y + r, 4)) for r in range(1, 4)]
    own = 2 * HOPS + core

    local = [
        pltpu.make_async_copy(k_ref.at[:, cols(y, HD)], kv.at[own, y, :, 0:HD], local_sem.at[0]),
        pltpu.make_async_copy(v_ref.at[:, cols(y, HD)], kv.at[own, y, :, HD:2 * HD], local_sem.at[1]),
        pltpu.make_async_copy(q_ref.at[:, cols(y, GROUP * HD)], qh.at[y], local_sem.at[2]),
        pltpu.make_async_copy(g_ref.at[:, cols(y, GROUP * HD)], gh.at[y], local_sem.at[3]),
    ]
    for copy in local:
        copy.start()

    barrier = pltpu.get_barrier_semaphore()
    partners = peers + [sibling, after, before]
    for partner in partners:
        pl.semaphore_signal(barrier, inc=1, device_id=partner, device_id_type=MESH)
    pl.semaphore_wait(barrier, len(partners))

    kv_copies, qg_copies, ring, sib = {}, {}, {}, {}
    for r in range(1, 4):
        for part, ref in enumerate((k_ref, v_ref)):
            kv_copies[r, part] = remote(
                ref.at[:, cols(peers[r - 1][1], HD)],
                kv.at[own, y, :, part * HD:(part + 1) * HD],
                kv_send.at[r - 1, part], kv_recv.at[r - 1, part], peers[r - 1],
            )
            kv_copies[r, part].start()

    def forward(distance, r):
        slot = lax.rem(y + 4 - r, 4)
        here = 2 * (HOPS - distance) + core
        if distance < HOPS:
            ring[distance, r] = remote(
                kv.at[here, slot], kv.at[here - 2, slot],
                ring_send.at[distance, r], ring_recv.at[distance, r], after,
            )
            ring[distance, r].start()
        sib[distance, r] = remote(
            kv.at[here, slot], kv.at[here, slot],
            sib_send.at[distance, r], sib_recv.at[distance, r], sibling,
        )
        sib[distance, r].start()

    def relay(distance, pieces):
        for r in pieces:
            ring[distance - 1, r].wait_recv()
            forward(distance, r)

    def from_sibling(b):
        at = b + core
        distance = HOPS - at // 2
        for r in range(4):
            slot = lax.rem(y + 4 - r, 4)
            remote(
                kv.at[at, slot], kv.at[at, slot],
                sib_send.at[distance, r], sib_recv.at[distance, r], sibling,
            ).wait_recv()

    local[0].wait()
    local[1].wait()
    forward(0, 0)
    for part, (ref, landing) in enumerate(((q_ref, qh), (g_ref, gh))):
        for r in range(1, 4):
            qg_copies[r, part] = remote(
                ref.at[:, cols(peers[r - 1][1], GROUP * HD)], landing.at[y],
                qg_send.at[r - 1, part], qg_recv.at[r - 1, part], peers[r - 1],
            )
            qg_copies[r, part].start()

    first = me * TOK - SPAN * TOK
    starts, positions = [], []
    for t in range(TILES):
        local_pos = lax.broadcasted_iota(jnp.int32, (1, TILE), 1) + (SPAN * TOK + t * TILE)
        begin = jnp.int32(0) - first
        start = jnp.zeros((1, TILE), jnp.int32) - first
        for d in range(NDOCS):
            start = jnp.where(local_pos >= begin, begin, start)
            begin = begin + len_ref[d]
        starts.append(jnp.concatenate([start] * GROUP, axis=1))
        positions.append(jnp.concatenate([local_pos] * GROUP, axis=1))

    for r in range(1, 4):
        kv_copies[r, 0].wait_recv()
        kv_copies[r, 1].wait_recv()
        forward(0, r)
    relay(1, (0, 1))
    local[2].wait()
    for r in range(1, 4):
        qg_copies[r, 0].wait_recv()
    for t in range(TILES):
        for h in range(GROUP):
            for s in range(TILE // SLOT):
                row = h * TILE + s * SLOT
                qs[t, row:row + SLOT, :] = qh[t * (TILE // SLOT) + s, :, h * HD:(h + 1) * HD]
    relay(1, (2, 3))

    def keys(u, part):
        at = u // 2 + core
        return kv[at, 2 * (u % 2):2 * (u % 2) + 2, :, part * HD:(part + 1) * HD].reshape(2 * SLOT, HD)

    def attend(group, t, subs):
        top = jnp.full((8, WIDTH), -1e30, F32)
        for n, u in enumerate(subs):
            s = over(keys(u, 0), qs[t], 1, 1)
            key_pos = lax.broadcasted_iota(jnp.int32, (TILE, WIDTH), 0) + u * TILE
            allowed = key_pos >= starts[t]
            if u == 2 * SPAN + t:
                allowed = allowed & (key_pos <= positions[t])
            s = jnp.where(allowed, s, -1e30)
            logits[n] = s
            top = jnp.maximum(top, jnp.max(s.reshape(TILE // 8, 8, WIDTH), axis=0))
        top = jnp.max(top, axis=0, keepdims=True) * SCALE2
        if group > 0:
            old = tops[group - 1, t, 0:1, :]
            top = jnp.maximum(top, old)
        tops[group, t] = jnp.broadcast_to(top, (8, WIDTH))
        norm = jnp.zeros((8, WIDTH), F32)
        out = jnp.zeros((HD, WIDTH), F32)
        for n, u in enumerate(subs):
            e = jnp.exp2(logits[n] * SCALE2 - top)
            norm = norm + jnp.sum(e.reshape(TILE // 8, 8, WIDTH), axis=0)
            e = e.astype(BF16)
            weights[t, u - t] = e
            out = out + over(keys(u, 1), e, 0, 0)
        if group > 0:
            fade = jnp.exp2(old - top)
            norm = norm + sums[t] * fade
            out = out + outs[t] * fade
        sums[t] = norm
        outs[t] = out

    attend(0, 0, (12,))
    attend(0, 1, (12, 13))
    from_sibling(5)
    attend(1, 0, (8, 9, 10, 11))
    relay(2, (0, 1))
    attend(1, 1, (8, 9, 10, 11))
    relay(2, (2, 3))
    from_sibling(3)
    attend(2, 0, (4, 5, 6, 7))
    relay(3, (0, 1))
    attend(2, 1, (4, 5, 6, 7))
    local[3].wait()
    for r in range(1, 4):
        qg_copies[r, 1].wait_recv()
    for t in range(TILES):
        for h in range(GROUP):
            for s in range(TILE // SLOT):
                row = h * TILE + s * SLOT
                gt[t, :, row:row + SLOT] = gh[t * (TILE // SLOT) + s, :, h * HD:(h + 1) * HD].T
    relay(3, (2, 3))
    from_sibling(1)
    attend(3, 0, (0, 1, 2, 3))
    attend(3, 1, (1, 2, 3))

    inverses = []
    for t in range(TILES):
        inverse = 1.0 / jnp.sum(sums[t], axis=0, keepdims=True)
        inverses.append(inverse)
        out = (outs[t] * inverse).astype(BF16)
        outs[t] = out.astype(F32)
        out_rows = out.T
        for h in range(GROUP):
            for s in range(TILE // SLOT):
                row = h * TILE + s * SLOT
                o_buf[t * (TILE // SLOT) + s, :, h * HD:(h + 1) * HD] = out_rows[row:row + SLOT, :]
    od = []

    def deliver(part, buf, result):
        for r in range(1, 4):
            od.append(remote(
                buf.at[peers[r - 1][1]], result.at[:, cols(y, GROUP * HD)],
                od_send.at[r - 1, part], od_recv.at[r - 1, part], peers[r - 1],
            ))
            od[-1].start()
        copy = pltpu.make_async_copy(buf.at[y], result.at[:, cols(y, GROUP * HD)], local_sem.at[4 + part])
        copy.start()
        local.append(copy)

    deliver(0, o_buf, att_ref)
    sib_in[HOPS * (1 - core)] = jnp.zeros_like(sib_in[0])
    dqs[...] = jnp.zeros_like(dqs)
    deltas = [None] * TILES

    def prepare(group):
        for t in range(TILES):
            factor = inverses[t]
            if group < HOPS:
                factor = factor * jnp.exp2(tops[group, t, 0:1, :] - tops[HOPS, t, 0:1, :])
            grad = (gt[t].astype(F32) * factor).astype(BF16)
            deltas[t] = jnp.sum(grad.astype(F32) * outs[t], axis=0, keepdims=True)
            gst[t] = grad
            gs[t] = grad.T

    def backward(u):
        dk = jnp.zeros((TILE, HD), F32)
        dv = jnp.zeros((TILE, HD), F32)
        for t in range(TILES):
            if 0 <= u - t <= 2 * SPAN:
                e = weights[t, u - t]
                dp = over(keys(u, 1), gst[t], 1, 0)
                ds = (e.astype(F32) * (dp - deltas[t])).astype(BF16)
                dk = dk + over(ds, qs[t], 1, 0)
                dv = dv + over(e, gs[t], 1, 0)
                dqs[t] += over(keys(u, 0), ds, 0, 0)
        return jnp.concatenate([dk * SCALE, dv], axis=1)

    back_sib, back = {}, {}

    def to_sibling(n, half):
        sib_out[n, half] = backward(2 * (2 * n + 1) + half).astype(BF16)
        back_sib[n, half] = remote(
            sib_out.at[n, half], sib_in.at[HOPS - n - core, half],
            back_sib_send.at[n, half], back_sib_recv.at[n, half], sibling,
        )
        back_sib[n, half].start()

    def back_ring(distance, half):
        value = backward(4 * (HOPS - distance) + half)
        back_sib[HOPS - distance, half].wait_recv()
        value = value + sib_in[distance, half].astype(F32)
        if distance < HOPS:
            back[distance + 1, half].wait_recv()
            value = value + ring_in[distance, half].astype(F32)
        ring_out[distance - 1, half] = value.astype(BF16)
        back[distance, half] = remote(
            ring_out.at[distance - 1, half], ring_in.at[distance - 1, half],
            back_send.at[distance - 1, half], back_recv.at[distance - 1, half], before,
        )
        back[distance, half].start()

    for n in range(HOPS):
        prepare(HOPS - n)
        for half in range(2):
            to_sibling(n, half)
            back_ring(HOPS - n, half)
    prepare(0)
    for half in range(2):
        own_buf[half] = backward(2 * SPAN + half)
    for t in range(TILES):
        dq_rows = (dqs[t] * SCALE).astype(BF16).T
        for h in range(GROUP):
            for s in range(TILE // SLOT):
                row = h * TILE + s * SLOT
                dq_buf[t * (TILE // SLOT) + s, :, h * HD:(h + 1) * HD] = dq_rows[row:row + SLOT, :]
    deliver(1, dq_buf, dqo_ref)
    for half in range(2):
        back[1, half].wait_recv()
        value = own_buf[half] + sib_in[0, half].astype(F32) + ring_in[0, half].astype(F32)
        final[2 * half:2 * half + 2] = value.astype(BF16).reshape(2, SLOT, 2 * HD)
    for r in range(1, 4):
        for part, result in enumerate((dk_ref, dv_ref)):
            od.append(remote(
                final.at[peers[r - 1][1], :, part * HD:(part + 1) * HD], result.at[:, cols(y, HD)],
                fin_send.at[r - 1, part], fin_recv.at[r - 1, part], peers[r - 1],
            ))
            od[-1].start()
    for part, result in enumerate((dk_ref, dv_ref)):
        copy = pltpu.make_async_copy(
            final.at[y, :, part * HD:(part + 1) * HD], result.at[:, cols(y, HD)], local_sem.at[6 + part]
        )
        copy.start()
        local.append(copy)

    for copy in local[4:]:
        copy.wait()
    for copies in (kv_copies, qg_copies, ring, sib, back_sib, back):
        for copy in copies.values():
            copy.wait_send()
    for r in range(4):
        distance = HOPS * core
        at = 2 * (HOPS - distance) + 1 - core
        slot = lax.rem(y + 4 - r, 4)
        remote(
            kv.at[at, slot], kv.at[at, slot], sib_send.at[distance, r], sib_recv.at[distance, r], sibling
        ).wait_recv()
    for copy in od:
        copy.wait()


def shards(queries, key_states, value_states, out_grad, lengths):
    hbm = pl.BlockSpec(memory_space=pl.ANY)
    smem = pl.BlockSpec(memory_space=pltpu.SMEM)
    dma = pltpu.SemaphoreType.DMA
    vmem = pltpu.VMEM
    by_head = (4, SLOT, GROUP * HD)
    half_block = (2, TILE, 2 * HD)
    return pl.pallas_call(
        kernel,
        name="attention",
        out_shape=(
            jax.ShapeDtypeStruct((SLOT, 4 * GROUP * HD), BF16),
            jax.ShapeDtypeStruct((SLOT, 4 * GROUP * HD), BF16),
            jax.ShapeDtypeStruct((SLOT, 4 * HD), BF16),
            jax.ShapeDtypeStruct((SLOT, 4 * HD), BF16),
        ),
        in_specs=[smem] + [hbm] * 4,
        out_specs=(hbm,) * 4,
        scratch_shapes=[
            vmem((2 * HOPS + 2, 4, SLOT, 2 * HD), BF16),
            vmem(by_head, BF16),
            vmem(by_head, BF16),
            vmem((TILES, WIDTH, HD), BF16),
            vmem((TILES, HD, WIDTH), BF16),
            vmem((TILES, 2 * SPAN + 1, TILE, WIDTH), BF16),
            vmem((4, TILE, WIDTH), F32),
            vmem((HOPS + 1, TILES, 8, WIDTH), F32),
            vmem((TILES, 8, WIDTH), F32),
            vmem((TILES, HD, WIDTH), F32),
            vmem((TILES, HD, WIDTH), F32),
            vmem((TILES, HD, WIDTH), BF16),
            vmem((TILES, WIDTH, HD), BF16),
            vmem(by_head, BF16),
            vmem(by_head, BF16),
            vmem((HOPS,) + half_block, BF16),
            vmem((HOPS + 1,) + half_block, BF16),
            vmem((HOPS,) + half_block, BF16),
            vmem((HOPS,) + half_block, BF16),
            vmem(half_block, F32),
            vmem((4, SLOT, 2 * HD), BF16),
            dma((8,)), dma((3, 2)), dma((3, 2)), dma((3, 2)), dma((3, 2)),
            dma((HOPS, 4)), dma((HOPS, 4)), dma((HOPS + 1, 4)), dma((HOPS + 1, 4)),
            dma((3, 2)), dma((3, 2)), dma((HOPS, 2)), dma((HOPS, 2)),
            dma((HOPS, 2)), dma((HOPS, 2)), dma((3, 2)), dma((3, 2)),
        ],
        compiler_params=pltpu.CompilerParams(
            collective_id=0, has_side_effects=True, vmem_limit_bytes=56 * 2**20
        ),
    )(lengths, queries, key_states, value_states, out_grad)


def solution(mesh):
    rows = P(("ctx", "head"), None)
    return jax.shard_map(
        shards, mesh=mesh, in_specs=(rows,) * 4 + (P(),), out_specs=(rows,) * 4, check_vma=False
    )
```

```python
import jax
import jax.numpy as jnp
import numpy as np
from jax import lax
from jax.experimental import pallas as pl
from jax.experimental.pallas import tpu as pltpu
from jax.sharding import PartitionSpec as P

HD = 128
SPAN = 6
TOK = 512
SLOT = 128
GROUP = 4
HOPS = 3
NDOCS = 21
PARTS = 2
TILE = 256
TILES = TOK // TILE
SUBS = 2 * (SPAN + 1)
WIDTH = GROUP * TILE
SCALE = HD ** (-0.5)
SCALE2 = float(HD ** (-0.5) * np.log2(np.e))
MESH = pl.DeviceIdType.MESH
BF16 = jnp.bfloat16
F32 = jnp.float32


def cols(index, width):
    return pl.ds(pl.multiple_of(index * width, width), width)


def over(left, right, a, b):
    return lax.dot_general(left, right, (((a,), (b,)), ((), ())), preferred_element_type=F32)


def remote(src, dst, send, recv, device):
    return pltpu.make_async_remote_copy(
        src_ref=src, dst_ref=dst, send_sem=send, recv_sem=recv, device_id=device, device_id_type=MESH
    )


def kernel(
    len_ref, q_ref, k_ref, v_ref, g_ref, att_ref, dqo_ref, dk_ref, dv_ref,
    kv, qh, gh, qs, gt, weights, logits, tops, sums, outs, dqs, gst, gs, slopes,
    o_buf, dq_buf, sib_out, sib_in, ring_out, ring_in, own_buf, final,
    local_sem, kv_send, kv_recv, qg_send, qg_recv, ring_send, ring_recv, sib_send, sib_recv,
    od_send, od_recv, back_sib_send, back_sib_recv, back_send, back_recv, fin_send, fin_recv,
):
    me = lax.axis_index("ctx")
    y = lax.axis_index("head")
    count = lax.axis_size("ctx")
    core = lax.rem(me, 2)
    sibling = (me + 1 - 2 * core, y)
    after = (lax.rem(me + 2, count), y)
    before = (lax.rem(me + count - 2, count), y)
    peers = [(me, lax.rem(y + r, 4)) for r in range(1, 4)]
    own = 2 * HOPS + core

    local = [
        pltpu.make_async_copy(k_ref.at[:, cols(y, HD)], kv.at[own, y, :, 0:HD], local_sem.at[0]),
        pltpu.make_async_copy(v_ref.at[:, cols(y, HD)], kv.at[own, y, :, HD:2 * HD], local_sem.at[1]),
        pltpu.make_async_copy(q_ref.at[:, cols(y, GROUP * HD)], qh.at[y], local_sem.at[2]),
        pltpu.make_async_copy(g_ref.at[:, cols(y, GROUP * HD)], gh.at[y], local_sem.at[3]),
    ]
    for copy in local:
        copy.start()

    barrier = pltpu.get_barrier_semaphore()
    partners = peers + [sibling, after, before]
    for partner in partners:
        pl.semaphore_signal(barrier, inc=1, device_id=partner, device_id_type=MESH)
    pl.semaphore_wait(barrier, len(partners))

    kv_copies, qg_copies, ring, sib = {}, {}, {}, {}
    for r in range(1, 4):
        for part, ref in enumerate((k_ref, v_ref)):
            kv_copies[r, part] = remote(
                ref.at[:, cols(peers[r - 1][1], HD)],
                kv.at[own, y, :, part * HD:(part + 1) * HD],
                kv_send.at[r - 1, part], kv_recv.at[r - 1, part], peers[r - 1],
            )
            kv_copies[r, part].start()

    def forward(distance, r):
        slot = lax.rem(y + 4 - r, 4)
        here = 2 * (HOPS - distance) + core
        if distance < HOPS:
            ring[distance, r] = remote(
                kv.at[here, slot], kv.at[here - 2, slot],
                ring_send.at[distance, r], ring_recv.at[distance, r], after,
            )
            ring[distance, r].start()
        sib[distance, r] = remote(
            kv.at[here, slot], kv.at[here, slot],
            sib_send.at[distance, r], sib_recv.at[distance, r], sibling,
        )
        sib[distance, r].start()

    def relay(distance, pieces):
        for r in pieces:
            ring[distance - 1, r].wait_recv()
            forward(distance, r)

    def from_sibling(b):
        at = b + core
        distance = HOPS - at // 2
        for r in range(4):
            slot = lax.rem(y + 4 - r, 4)
            remote(
                kv.at[at, slot], kv.at[at, slot],
                sib_send.at[distance, r], sib_recv.at[distance, r], sibling,
            ).wait_recv()

    local[0].wait()
    local[1].wait()
    forward(0, 0)
    for part, (ref, landing) in enumerate(((q_ref, qh), (g_ref, gh))):
        for r in range(1, 4):
            qg_copies[r, part] = remote(
                ref.at[:, cols(peers[r - 1][1], GROUP * HD)], landing.at[y],
                qg_send.at[r - 1, part], qg_recv.at[r - 1, part], peers[r - 1],
            )
            qg_copies[r, part].start()

    first = me * TOK - SPAN * TOK
    starts, positions = [], []
    for t in range(TILES):
        local_pos = lax.broadcasted_iota(jnp.int32, (1, TILE), 1) + (SPAN * TOK + t * TILE)
        begin = jnp.int32(0) - first
        start = jnp.zeros((1, TILE), jnp.int32) - first
        for d in range(NDOCS):
            start = jnp.where(local_pos >= begin, begin, start)
            begin = begin + len_ref[d]
        starts.append(jnp.concatenate([start] * GROUP, axis=1))
        positions.append(jnp.concatenate([local_pos] * GROUP, axis=1))

    for r in range(1, 4):
        kv_copies[r, 0].wait_recv()
        kv_copies[r, 1].wait_recv()
        forward(0, r)
    relay(1, (0, 1, 2, 3))
    local[2].wait()
    for r in range(1, 4):
        qg_copies[r, 0].wait_recv()
    for t in range(TILES):
        for h in range(GROUP):
            for s in range(TILE // SLOT):
                row = h * TILE + s * SLOT
                qs[t, row:row + SLOT, :] = qh[t * (TILE // SLOT) + s, :, h * HD:(h + 1) * HD]

    def keys(u, part):
        at = u // 2 + core
        return kv[at, 2 * (u % 2):2 * (u % 2) + 2, :, part * HD:(part + 1) * HD].reshape(2 * SLOT, HD)

    def scores(t, subs, top):
        for u in subs:
            s = over(keys(u, 0), qs[t], 1, 1)
            key_pos = lax.broadcasted_iota(jnp.int32, (TILE, WIDTH), 0) + u * TILE
            allowed = key_pos >= starts[t]
            if u == 2 * SPAN + t:
                allowed = allowed & (key_pos <= positions[t])
            s = jnp.where(allowed, s, -1e30)
            logits[t, u % 4] = s
            top = jnp.maximum(top, jnp.max(s.reshape(TILE // 8, 8, WIDTH), axis=0))
        return top

    lowest = jnp.full((8, WIDTH), -1e30, F32)

    def attend(group, t, subs):
        mix(group, t, subs, scores(t, subs, lowest))

    def mix(group, t, subs, top):
        top = jnp.max(top, axis=0, keepdims=True) * SCALE2
        if group > 0:
            old = tops[group - 1, t, 0:1, :]
            top = jnp.maximum(top, old)
        tops[group, t] = jnp.broadcast_to(top, (8, WIDTH))
        norm = jnp.zeros((8, WIDTH), F32)
        out = jnp.zeros((HD, WIDTH), F32)
        for u in subs:
            e = jnp.exp2(logits[t, u % 4] * SCALE2 - top)
            norm = norm + jnp.sum(e.reshape(TILE // 8, 8, WIDTH), axis=0)
            e = e.astype(BF16)
            weights[t, u - t] = e
            out = out + over(keys(u, 1), e, 0, 0)
        if group > 0:
            fade = jnp.exp2(old - top)
            norm = norm + sums[t] * fade
            out = out + outs[t] * fade
        sums[t] = norm
        outs[t] = out

    attend(0, 0, (12,))
    attend(0, 1, (12, 13))
    from_sibling(5)
    attend(1, 0, (8, 9, 10, 11))
    relay(2, (0, 1))
    attend(1, 1, (8, 9, 10, 11))
    relay(2, (2, 3))
    from_sibling(3)
    attend(2, 0, (4, 5, 6, 7))
    relay(3, (0, 1))
    attend(2, 1, (4, 5, 6, 7))
    local[3].wait()
    for r in range(1, 4):
        qg_copies[r, 1].wait_recv()
    for t in range(TILES):
        for h in range(GROUP):
            for s in range(TILE // SLOT):
                row = h * TILE + s * SLOT
                gt[t, :, row:row + SLOT] = gh[t * (TILE // SLOT) + s, :, h * HD:(h + 1) * HD].T
    relay(3, (2, 3))
    partial = [scores(0, (0, 1), lowest), scores(1, (1,), lowest)]
    from_sibling(1)
    mix(3, 0, (0, 1, 2, 3), scores(0, (2, 3), partial[0]))
    mix(3, 1, (1, 2, 3), scores(1, (2, 3), partial[1]))

    inverses = []
    for t in range(TILES):
        inverse = 1.0 / jnp.sum(sums[t], axis=0, keepdims=True)
        inverses.append(inverse)
        out = (outs[t] * inverse).astype(BF16)
        outs[t] = out.astype(F32)
    od = []

    def deliver(part, buf, result):
        for r in range(1, 4):
            od.append(remote(
                buf.at[peers[r - 1][1]], result.at[:, cols(y, GROUP * HD)],
                od_send.at[r - 1, part], od_recv.at[r - 1, part], peers[r - 1],
            ))
            od[-1].start()
        copy = pltpu.make_async_copy(buf.at[y], result.at[:, cols(y, GROUP * HD)], local_sem.at[4 + part])
        copy.start()
        local.append(copy)

    def fill(buf, t, value):
        rows = value.astype(BF16).T
        for h in range(GROUP):
            for s in range(TILE // SLOT):
                row = h * TILE + s * SLOT
                buf[t * (TILE // SLOT) + s, :, h * HD:(h + 1) * HD] = rows[row:row + SLOT, :]

    sib_in[HOPS * (1 - core)] = jnp.zeros_like(sib_in[0])
    dqs[...] = jnp.zeros_like(dqs)
    deltas = [None] * TILES

    def prepare(group):
        for t in range(TILES):
            factor = inverses[t]
            if group < HOPS:
                factor = factor * jnp.exp2(tops[group, t, 0:1, :] - tops[HOPS, t, 0:1, :])
            grad = (gt[t].astype(F32) * factor).astype(BF16)
            deltas[t] = jnp.sum(grad.astype(F32) * outs[t], axis=0, keepdims=True)
            gst[t] = grad
            gs[t] = grad.T

    def backward(u):
        tiles = [t for t in range(TILES) if 0 <= u - t <= 2 * SPAN]
        for t in tiles:
            dp = over(keys(u, 1), gst[t], 1, 0)
            slopes[t] = (weights[t, u - t].astype(F32) * (dp - deltas[t])).astype(BF16)
        dk = sum(over(slopes[t], qs[t], 1, 0) for t in tiles)
        dv = sum(over(weights[t, u - t], gs[t], 1, 0) for t in tiles)
        for t in tiles:
            dqs[t] += over(keys(u, 0), slopes[t], 0, 0)
        return jnp.concatenate([dk * SCALE, dv], axis=1)

    back_sib, back = {}, {}

    def to_sibling(n, half):
        sib_out[n, half] = backward(2 * (2 * n + 1) + half).astype(BF16)
        back_sib[n, half] = remote(
            sib_out.at[n, half], sib_in.at[HOPS - n - core, half],
            back_sib_send.at[n, half], back_sib_recv.at[n, half], sibling,
        )
        back_sib[n, half].start()

    def back_ring(distance, half):
        value = backward(4 * (HOPS - distance) + half)
        back_sib[HOPS - distance, half].wait_recv()
        value = value + sib_in[distance, half].astype(F32)
        if distance < HOPS:
            back[distance + 1, half].wait_recv()
            value = value + ring_in[distance, half].astype(F32)
        ring_out[distance - 1, half] = value.astype(BF16)
        back[distance, half] = remote(
            ring_out.at[distance - 1, half], ring_in.at[distance - 1, half],
            back_send.at[distance - 1, half], back_recv.at[distance - 1, half], before,
        )
        back[distance, half].start()

    for n in range(HOPS):
        prepare(HOPS - n)
        for half in range(2):
            to_sibling(n, half)
            back_ring(HOPS - n, half)
        if n == 0:
            for t in range(TILES):
                fill(o_buf, t, outs[t])
            deliver(0, o_buf, att_ref)
    prepare(0)
    for half in range(2):
        own_buf[half] = backward(2 * SPAN + half)
    for t in range(TILES):
        fill(dq_buf, t, dqs[t] * SCALE)
    deliver(1, dq_buf, dqo_ref)

    def give(slot, part, source, away):
        result = (dk_ref, dv_ref)[part]
        src = final.at[slot, :, part * HD:(part + 1) * HD]
        dst = result.at[:, cols(source, HD)]
        if away:
            return remote(src, dst, fin_send.at[slot, part], fin_recv.at[source, part], (me, slot))
        return pltpu.make_async_copy(src, dst, local_sem.at[6 + part])

    for half in range(2):
        back[1, half].wait_recv()
        value = own_buf[half] + sib_in[0, half].astype(F32) + ring_in[0, half].astype(F32)
        final[2 * half:2 * half + 2] = value.astype(BF16).reshape(2, SLOT, 2 * HD)
        for slot in (2 * half, 2 * half + 1):

            @pl.when(y != slot)
            def _():
                for part in range(2):
                    give(slot, part, y, True).start()

            @pl.when(y == slot)
            def _():
                for part in range(2):
                    give(slot, part, y, False).start()

    for copy in local[4:]:
        copy.wait()
    for copies in (kv_copies, qg_copies, ring, sib, back_sib, back):
        for copy in copies.values():
            copy.wait_send()
    for r in range(4):
        distance = HOPS * core
        at = 2 * (HOPS - distance) + 1 - core
        slot = lax.rem(y + 4 - r, 4)
        remote(
            kv.at[at, slot], kv.at[at, slot], sib_send.at[distance, r], sib_recv.at[distance, r], sibling
        ).wait_recv()
    for copy in od:
        copy.wait()
    for slot in range(4):

        @pl.when(y != slot)
        def _():
            for part in range(2):
                give(slot, part, y, True).wait_send()
                give(slot, part, slot, True).wait_recv()

        @pl.when(y == slot)
        def _():
            for part in range(2):
                give(slot, part, y, False).wait()


def place_kernel(*refs):
    ins, outs, bufs, sems = refs[:4], refs[4:8], refs[8:12], refs[12]
    rows = SLOT // PARTS
    loads, stores = [], []
    for n in range(4):
        for p in range(PARTS):
            part = pl.ds(p * rows, rows)
            loads.append(pltpu.make_async_copy(ins[n].at[part], bufs[n].at[part], sems.at[0, n, p]))
            stores.append(pltpu.make_async_copy(bufs[n].at[part], outs[n].at[part], sems.at[1, n, p]))
    for copy in loads:
        copy.start()
    for load, store in zip(loads, stores):
        load.wait()
        store.start()
    for copy in stores:
        copy.wait()


def shards(queries, key_states, value_states, out_grad, lengths):
    hbm = pl.BlockSpec(memory_space=pl.ANY)
    smem = pl.BlockSpec(memory_space=pltpu.SMEM)
    dma = pltpu.SemaphoreType.DMA
    vmem = pltpu.VMEM
    by_head = (4, SLOT, GROUP * HD)
    half_block = (2, TILE, 2 * HD)
    out_shape = (
        jax.ShapeDtypeStruct((SLOT, 4 * GROUP * HD), BF16),
        jax.ShapeDtypeStruct((SLOT, 4 * GROUP * HD), BF16),
        jax.ShapeDtypeStruct((SLOT, 4 * HD), BF16),
        jax.ShapeDtypeStruct((SLOT, 4 * HD), BF16),
    )
    results = pl.pallas_call(
        kernel,
        name="attention",
        out_shape=out_shape,
        in_specs=[smem] + [hbm] * 4,
        out_specs=(hbm,) * 4,
        scratch_shapes=[
            vmem((2 * HOPS + 2, 4, SLOT, 2 * HD), BF16),
            vmem(by_head, BF16),
            vmem(by_head, BF16),
            vmem((TILES, WIDTH, HD), BF16),
            vmem((TILES, HD, WIDTH), BF16),
            vmem((TILES, 2 * SPAN + 1, TILE, WIDTH), BF16),
            vmem((TILES, 4, TILE, WIDTH), F32),
            vmem((HOPS + 1, TILES, 8, WIDTH), F32),
            vmem((TILES, 8, WIDTH), F32),
            vmem((TILES, HD, WIDTH), F32),
            vmem((TILES, HD, WIDTH), F32),
            vmem((TILES, HD, WIDTH), BF16),
            vmem((TILES, WIDTH, HD), BF16),
            vmem((TILES, TILE, WIDTH), BF16),
            vmem(by_head, BF16),
            vmem(by_head, BF16),
            vmem((HOPS,) + half_block, BF16),
            vmem((HOPS + 1,) + half_block, BF16),
            vmem((HOPS,) + half_block, BF16),
            vmem((HOPS,) + half_block, BF16),
            vmem(half_block, F32),
            vmem((4, SLOT, 2 * HD), BF16),
            dma((8,)), dma((3, 2)), dma((3, 2)), dma((3, 2)), dma((3, 2)),
            dma((HOPS, 4)), dma((HOPS, 4)), dma((HOPS + 1, 4)), dma((HOPS + 1, 4)),
            dma((3, 2)), dma((3, 2)), dma((HOPS, 2)), dma((HOPS, 2)),
            dma((HOPS, 2)), dma((HOPS, 2)), dma((4, 2)), dma((4, 2)),
        ],
        compiler_params=pltpu.CompilerParams(
            collective_id=0, has_side_effects=True, vmem_limit_bytes=56 * 2**20
        ),
    )(lengths, queries, key_states, value_states, out_grad)
    return pl.pallas_call(
        place_kernel,
        name="place",
        out_shape=out_shape,
        in_specs=[hbm] * 4,
        out_specs=(hbm,) * 4,
        scratch_shapes=[vmem(out.shape, BF16) for out in out_shape] + [dma((2, 4, PARTS))],
    )(*results)


def solution(mesh):
    rows = P(("ctx", "head"), None)
    return jax.shard_map(
        shards, mesh=mesh, in_specs=(rows,) * 4 + (P(),), out_specs=(rows,) * 4, check_vma=False
    )
```

```python
import jax
import jax.numpy as jnp
import numpy as np
from jax import lax
from jax.experimental import pallas as pl
from jax.experimental.pallas import tpu as pltpu
from jax.sharding import PartitionSpec as P

HD = 128
SPAN = 6
TOK = 512
SLOT = 128
GROUP = 4
HOPS = 3
NDOCS = 21
PARTS = 2
TILE = 256
TILES = TOK // TILE
SUBS = 2 * (SPAN + 1)
WIDTH = GROUP * TILE
SCALE = HD ** (-0.5)
SCALE2 = float(HD ** (-0.5) * np.log2(np.e))
MESH = pl.DeviceIdType.MESH
BF16 = jnp.bfloat16
F32 = jnp.float32


def cols(index, width):
    return pl.ds(pl.multiple_of(index * width, width), width)


def over(left, right, a, b):
    return lax.dot_general(left, right, (((a,), (b,)), ((), ())), preferred_element_type=F32)


def remote(src, dst, send, recv, device):
    return pltpu.make_async_remote_copy(
        src_ref=src, dst_ref=dst, send_sem=send, recv_sem=recv, device_id=device, device_id_type=MESH
    )


def kernel(
    len_ref, q_ref, k_ref, v_ref, g_ref, att_ref, dqo_ref, dk_ref, dv_ref,
    kv, qh, gh, qs, qt, gq, weights, logits, begins, tops, sums, outs, inverse, dqs, gst, gs, deltas, slopes,
    o_buf, dq_buf, sib_out, sib_in, ring_out, ring_in, own_buf, final,
    local_sem, kv_send, kv_recv, qg_send, qg_recv, ring_send, ring_recv, sib_send, sib_recv,
    od_send, od_recv, back_sib_send, back_sib_recv, back_send, back_recv, fin_send, fin_recv,
):
    me = lax.axis_index("ctx")
    y = lax.axis_index("head")
    count = lax.axis_size("ctx")
    core = lax.rem(me, 2)
    sibling = (me + 1 - 2 * core, y)
    after = (lax.rem(me + 2, count), y)
    before = (lax.rem(me + count - 2, count), y)
    peers = [(me, lax.rem(y + r, 4)) for r in range(1, 4)]
    own = 2 * HOPS + core

    local = [
        pltpu.make_async_copy(k_ref.at[:, cols(y, HD)], kv.at[own, y, :, 0:HD], local_sem.at[0]),
        pltpu.make_async_copy(v_ref.at[:, cols(y, HD)], kv.at[own, y, :, HD:2 * HD], local_sem.at[1]),
        pltpu.make_async_copy(q_ref.at[:, cols(y, GROUP * HD)], qh.at[y], local_sem.at[2]),
        pltpu.make_async_copy(g_ref.at[:, cols(y, GROUP * HD)], gh.at[y], local_sem.at[3]),
    ]
    for copy in local:
        copy.start()

    barrier = pltpu.get_barrier_semaphore()
    partners = peers + [sibling, after, before]
    for partner in partners:
        pl.semaphore_signal(barrier, inc=1, device_id=partner, device_id_type=MESH)
    pl.semaphore_wait(barrier, len(partners))

    kv_copies, qg_copies, ring, sib = {}, {}, {}, {}
    for r in range(1, 4):
        for part, ref in enumerate((k_ref, v_ref)):
            kv_copies[r, part] = remote(
                ref.at[:, cols(peers[r - 1][1], HD)],
                kv.at[own, y, :, part * HD:(part + 1) * HD],
                kv_send.at[r - 1, part], kv_recv.at[r - 1, part], peers[r - 1],
            )
            kv_copies[r, part].start()

    def forward(distance, r):
        slot = lax.rem(y + 4 - r, 4)
        here = 2 * (HOPS - distance) + core
        if distance < HOPS:
            ring[distance, r] = remote(
                kv.at[here, slot], kv.at[here - 2, slot],
                ring_send.at[distance, r], ring_recv.at[distance, r], after,
            )
            ring[distance, r].start()
        sib[distance, r] = remote(
            kv.at[here, slot], kv.at[here, slot],
            sib_send.at[distance, r], sib_recv.at[distance, r], sibling,
        )
        sib[distance, r].start()

    def relay(distance, pieces):
        for r in pieces:
            ring[distance - 1, r].wait_recv()
            forward(distance, r)

    def from_sibling(b):
        at = b + core
        distance = HOPS - at // 2
        for r in range(4):
            slot = lax.rem(y + 4 - r, 4)
            remote(
                kv.at[at, slot], kv.at[at, slot],
                sib_send.at[distance, r], sib_recv.at[distance, r], sibling,
            ).wait_recv()

    local[0].wait()
    local[1].wait()
    forward(0, 0)
    for part, (ref, landing) in enumerate(((q_ref, qh), (g_ref, gh))):
        for r in range(1, 4):
            qg_copies[r, part] = remote(
                ref.at[:, cols(peers[r - 1][1], GROUP * HD)], landing.at[y],
                qg_send.at[r - 1, part], qg_recv.at[r - 1, part], peers[r - 1],
            )
            qg_copies[r, part].start()

    first = me * TOK - SPAN * TOK
    for t in range(TILES):
        local_pos = lax.broadcasted_iota(jnp.int32, (TILE, HD), 0) + (SPAN * TOK + t * TILE)
        begin = jnp.int32(0) - first
        start = jnp.zeros((TILE, HD), jnp.int32) - first
        for d in range(NDOCS):
            start = jnp.where(local_pos >= begin, begin, start)
            begin = begin + len_ref[d]
        for h in range(GROUP):
            begins[t, h * TILE:(h + 1) * TILE, :] = start

    def unpack(t, source, rows):
        for h in range(GROUP):
            for s in range(TILE // SLOT):
                row = h * TILE + s * SLOT
                rows[t, row:row + SLOT, :] = source[t * (TILE // SLOT) + s, :, h * HD:(h + 1) * HD]

    for r in range(1, 4):
        kv_copies[r, 0].wait_recv()
        kv_copies[r, 1].wait_recv()
        forward(0, r)
    relay(1, (0, 1, 2, 3))
    local[2].wait()
    for r in range(1, 4):
        qg_copies[r, 0].wait_recv()
    for t in range(TILES):
        unpack(t, qh, qs)

    def keys(u, part):
        at = u // 2 + core
        return kv[at, 2 * (u % 2):2 * (u % 2) + 2, :, part * HD:(part + 1) * HD].reshape(2 * SLOT, HD)

    def twice(value):
        return jnp.concatenate([value, value], axis=1)

    def scores(t, subs, top):
        for u in subs:
            s = over(qs[t], keys(u, 0), 1, 1)
            key_pos = lax.broadcasted_iota(jnp.int32, (WIDTH, TILE), 1) + u * TILE
            allowed = key_pos >= twice(begins[t])
            if u == 2 * SPAN + t:
                row = lax.broadcasted_iota(jnp.int32, (WIDTH, TILE), 0)
                allowed = allowed & (key_pos <= (row & (TILE - 1)) + u * TILE)
            s = jnp.where(allowed, s, -1e30)
            logits[t, u % 4] = s
            top = jnp.maximum(top, jnp.maximum(s[:, :HD], s[:, HD:]))
        return top

    lowest = jnp.full((WIDTH, HD), -1e30, F32)

    def attend(group, t, subs):
        mix(group, t, subs, scores(t, subs, lowest))

    def mix(group, t, subs, top):
        top = jnp.broadcast_to(jnp.max(top, axis=1, keepdims=True) * SCALE2, (WIDTH, HD))
        if group > 0:
            old = tops[group - 1, t]
            top = jnp.maximum(top, old)
        tops[group, t] = top
        norm = jnp.zeros((WIDTH, HD), F32)
        out = jnp.zeros((WIDTH, HD), F32)
        for u in subs:
            e = jnp.exp2(logits[t, u % 4] * SCALE2 - twice(top))
            norm = norm + e[:, :HD] + e[:, HD:]
            e = e.astype(BF16)
            weights[t, u - t] = e
            out = out + over(e, keys(u, 1), 1, 0)
        if group > 0:
            fade = jnp.exp2(old - top)
            norm = norm + sums[t] * fade
            out = out + outs[t] * fade
        sums[t] = norm
        outs[t] = out

    attend(0, 0, (12,))
    attend(0, 1, (12, 13))
    from_sibling(5)
    attend(1, 0, (8, 9, 10, 11))
    relay(2, (0, 1))
    attend(1, 1, (8, 9, 10, 11))
    relay(2, (2, 3))
    from_sibling(3)
    attend(2, 0, (4, 5, 6, 7))
    relay(3, (0, 1))
    attend(2, 1, (4, 5, 6, 7))
    local[3].wait()
    for r in range(1, 4):
        qg_copies[r, 1].wait_recv()
    for t in range(TILES):
        unpack(t, gh, gq)
        qt[t] = qs[t].T
    relay(3, (2, 3))
    partial = [scores(0, (0, 1), lowest), scores(1, (1,), lowest)]
    from_sibling(1)
    mix(3, 0, (0, 1, 2, 3), scores(0, (2, 3), partial[0]))
    mix(3, 1, (1, 2, 3), scores(1, (2, 3), partial[1]))

    for t in range(TILES):
        total = jnp.sum(sums[t], axis=1, keepdims=True)
        inverse[t] = jnp.broadcast_to(1.0 / total, (WIDTH, HD))
        outs[t] = (outs[t] * inverse[t]).astype(BF16).astype(F32)
    od = []

    def deliver(part, buf, result):
        for r in range(1, 4):
            od.append(remote(
                buf.at[peers[r - 1][1]], result.at[:, cols(y, GROUP * HD)],
                od_send.at[r - 1, part], od_recv.at[r - 1, part], peers[r - 1],
            ))
            od[-1].start()
        copy = pltpu.make_async_copy(buf.at[y], result.at[:, cols(y, GROUP * HD)], local_sem.at[4 + part])
        copy.start()
        local.append(copy)

    def fill(buf, t, value):
        rows = value.astype(BF16)
        for h in range(GROUP):
            for s in range(TILE // SLOT):
                row = h * TILE + s * SLOT
                buf[t * (TILE // SLOT) + s, :, h * HD:(h + 1) * HD] = rows[row:row + SLOT, :]

    sib_in[HOPS * (1 - core)] = jnp.zeros_like(sib_in[0])
    dqs[...] = jnp.zeros_like(dqs)

    def prepare(group):
        for t in range(TILES):
            factor = inverse[t]
            if group < HOPS:
                factor = factor * jnp.exp2(tops[group, t] - tops[HOPS, t])
            grad = (gq[t].astype(F32) * factor).astype(BF16)
            delta = jnp.sum(grad.astype(F32) * outs[t], axis=1, keepdims=True)
            deltas[t] = jnp.broadcast_to(delta, (WIDTH, HD))
            gs[t] = grad
            gst[t] = grad.T

    def backward(u):
        tiles = [t for t in range(TILES) if 0 <= u - t <= 2 * SPAN]
        for t in tiles:
            dp = over(gs[t], keys(u, 1), 1, 1)
            slopes[t] = (weights[t, u - t].astype(F32) * (dp - twice(deltas[t]))).astype(BF16)
        dk = sum(over(qt[t], slopes[t], 1, 0) for t in tiles)
        dv = sum(over(gst[t], weights[t, u - t], 1, 0) for t in tiles)
        for t in tiles:
            dqs[t] += over(slopes[t], keys(u, 0), 1, 0)
        return jnp.concatenate([dk * SCALE, dv], axis=0).T

    back_sib, back = {}, {}

    def to_sibling(n, half):
        sib_out[n, half] = backward(2 * (2 * n + 1) + half).astype(BF16)
        back_sib[n, half] = remote(
            sib_out.at[n, half], sib_in.at[HOPS - n - core, half],
            back_sib_send.at[n, half], back_sib_recv.at[n, half], sibling,
        )
        back_sib[n, half].start()

    def back_ring(distance, half):
        value = backward(4 * (HOPS - distance) + half)
        back_sib[HOPS - distance, half].wait_recv()
        value = value + sib_in[distance, half].astype(F32)
        if distance < HOPS:
            back[distance + 1, half].wait_recv()
            value = value + ring_in[distance, half].astype(F32)
        ring_out[distance - 1, half] = value.astype(BF16)
        back[distance, half] = remote(
            ring_out.at[distance - 1, half], ring_in.at[distance - 1, half],
            back_send.at[distance - 1, half], back_recv.at[distance - 1, half], before,
        )
        back[distance, half].start()

    for n in range(HOPS):
        prepare(HOPS - n)
        for half in range(2):
            to_sibling(n, half)
        for half in range(2):
            back_ring(HOPS - n, half)
        if n == 0:
            for t in range(TILES):
                fill(o_buf, t, outs[t])
            deliver(0, o_buf, att_ref)
    prepare(0)
    for half in range(2):
        own_buf[half] = backward(2 * SPAN + half)
    for t in range(TILES):
        fill(dq_buf, t, dqs[t] * SCALE)
    deliver(1, dq_buf, dqo_ref)

    def give(slot, part, source, away):
        result = (dk_ref, dv_ref)[part]
        src = final.at[slot, :, part * HD:(part + 1) * HD]
        dst = result.at[:, cols(source, HD)]
        if away:
            return remote(src, dst, fin_send.at[slot, part], fin_recv.at[source, part], (me, slot))
        return pltpu.make_async_copy(src, dst, local_sem.at[6 + part])

    for half in range(2):
        back[1, half].wait_recv()
        value = own_buf[half] + sib_in[0, half].astype(F32) + ring_in[0, half].astype(F32)
        final[2 * half:2 * half + 2] = value.astype(BF16).reshape(2, SLOT, 2 * HD)
        for slot in (2 * half, 2 * half + 1):

            @pl.when(y != slot)
            def _():
                for part in range(2):
                    give(slot, part, y, True).start()

            @pl.when(y == slot)
            def _():
                for part in range(2):
                    give(slot, part, y, False).start()

    for copy in local[4:]:
        copy.wait()
    for copies in (kv_copies, qg_copies, ring, sib, back_sib, back):
        for copy in copies.values():
            copy.wait_send()
    for r in range(4):
        distance = HOPS * core
        at = 2 * (HOPS - distance) + 1 - core
        slot = lax.rem(y + 4 - r, 4)
        remote(
            kv.at[at, slot], kv.at[at, slot], sib_send.at[distance, r], sib_recv.at[distance, r], sibling
        ).wait_recv()
    for copy in od:
        copy.wait()
    for slot in range(4):

        @pl.when(y != slot)
        def _():
            for part in range(2):
                give(slot, part, y, True).wait_send()
                give(slot, part, slot, True).wait_recv()

        @pl.when(y == slot)
        def _():
            for part in range(2):
                give(slot, part, y, False).wait()


def place_kernel(*refs):
    ins, outs, bufs, sems = refs[:4], refs[4:8], refs[8:12], refs[12]
    rows = SLOT // PARTS
    loads, stores = [], []
    for n in range(4):
        for p in range(PARTS):
            part = pl.ds(p * rows, rows)
            loads.append(pltpu.make_async_copy(ins[n].at[part], bufs[n].at[part], sems.at[0, n, p]))
            stores.append(pltpu.make_async_copy(bufs[n].at[part], outs[n].at[part], sems.at[1, n, p]))
    for copy in loads:
        copy.start()
    for load, store in zip(loads, stores):
        load.wait()
        store.start()
    for copy in stores:
        copy.wait()


def shards(queries, key_states, value_states, out_grad, lengths):
    hbm = pl.BlockSpec(memory_space=pl.ANY)
    smem = pl.BlockSpec(memory_space=pltpu.SMEM)
    dma = pltpu.SemaphoreType.DMA
    vmem = pltpu.VMEM
    by_head = (4, SLOT, GROUP * HD)
    half_block = (2, TILE, 2 * HD)
    out_shape = (
        jax.ShapeDtypeStruct((SLOT, 4 * GROUP * HD), BF16),
        jax.ShapeDtypeStruct((SLOT, 4 * GROUP * HD), BF16),
        jax.ShapeDtypeStruct((SLOT, 4 * HD), BF16),
        jax.ShapeDtypeStruct((SLOT, 4 * HD), BF16),
    )
    results = pl.pallas_call(
        kernel,
        name="attention",
        out_shape=out_shape,
        in_specs=[smem] + [hbm] * 4,
        out_specs=(hbm,) * 4,
        scratch_shapes=[
            vmem((2 * HOPS + 2, 4, SLOT, 2 * HD), BF16),
            vmem(by_head, BF16),
            vmem(by_head, BF16),
            vmem((TILES, WIDTH, HD), BF16),
            vmem((TILES, HD, WIDTH), BF16),
            vmem((TILES, WIDTH, HD), BF16),
            vmem((TILES, 2 * SPAN + 1, WIDTH, TILE), BF16),
            vmem((TILES, 4, WIDTH, TILE), F32),
            vmem((TILES, WIDTH, HD), jnp.int32),
            vmem((HOPS + 1, TILES, WIDTH, HD), F32),
            vmem((TILES, WIDTH, HD), F32),
            vmem((TILES, WIDTH, HD), F32),
            vmem((TILES, WIDTH, HD), F32),
            vmem((TILES, WIDTH, HD), F32),
            vmem((TILES, HD, WIDTH), BF16),
            vmem((TILES, WIDTH, HD), BF16),
            vmem((TILES, WIDTH, HD), F32),
            vmem((TILES, WIDTH, TILE), BF16),
            vmem(by_head, BF16),
            vmem(by_head, BF16),
            vmem((HOPS,) + half_block, BF16),
            vmem((HOPS + 1,) + half_block, BF16),
            vmem((HOPS,) + half_block, BF16),
            vmem((HOPS,) + half_block, BF16),
            vmem(half_block, F32),
            vmem((4, SLOT, 2 * HD), BF16),
            dma((8,)), dma((3, 2)), dma((3, 2)), dma((3, 2)), dma((3, 2)),
            dma((HOPS, 4)), dma((HOPS, 4)), dma((HOPS + 1, 4)), dma((HOPS + 1, 4)),
            dma((3, 2)), dma((3, 2)), dma((HOPS, 2)), dma((HOPS, 2)),
            dma((HOPS, 2)), dma((HOPS, 2)), dma((4, 2)), dma((4, 2)),
        ],
        compiler_params=pltpu.CompilerParams(
            collective_id=0, has_side_effects=True, vmem_limit_bytes=56 * 2**20
        ),
    )(lengths, queries, key_states, value_states, out_grad)
    return pl.pallas_call(
        place_kernel,
        name="place",
        out_shape=out_shape,
        in_specs=[hbm] * 4,
        out_specs=(hbm,) * 4,
        scratch_shapes=[vmem(out.shape, BF16) for out in out_shape] + [dma((2, 4, PARTS))],
    )(*results)


def solution(mesh):
    rows = P(("ctx", "head"), None)
    return jax.shard_map(
        shards, mesh=mesh, in_specs=(rows,) * 4 + (P(),), out_specs=(rows,) * 4, check_vma=False
    )
```
